32 devices in a mesh: seq: 4 (over x, core), hid: 8 (over z, y).
Axes of the slice: x: 2, y: 2, z: 4, core: 2. Of those that a mesh axis runs over, the one named last changes fastest.
Arguments:
- stream: bfloat16 [2048, 2048], P('seq'), may hold values from -5 to 5
- queries: bfloat16 [2048, 16, 128], P('seq', 'hid'), may hold values from -150 to 150
- key_rows: bfloat16 [2048, 16, 128], P('seq', 'hid'), may hold values from -5 to 5
- value_rows: bfloat16 [2048, 16, 128], P('seq', 'hid'), may hold values from -5 to 5
- segment_ids: int32 [2048], replicated, may hold values from 0 to 3, never falling along the last dimension, each value on 1 to 1024 neighbouring positions
- out_proj: bfloat16 [16, 128, 2048], P('hid'), may hold values from -0.125 to 0.125
- norm_gain: float32 [2048], replicated, may hold values from 0.1 to 1.9
- expert_ids: int32 [2048, 6], P('seq'), may hold values from 0 to 63, all different within a row; in each aligned block of 512 rows (0 to 511, 512 to 1023, ...) at most 64 rows name the same one
- route_gates: float32 [2048, 6], P('seq'), may hold values from 0.05 to 0.4
- gate_proj: bfloat16 [90112, 2048], P(('seq', 'hid')), may hold values from -0.125 to 0.125
- up_proj: bfloat16 [90112, 2048], P(('seq', 'hid')), may hold values from -0.125 to 0.125
- down_proj: bfloat16 [90112, 2048], P(('seq', 'hid')), may hold values from -0.15625 to 0.15625
- shared_gate: bfloat16 [2816, 2048], P('hid'), may hold values from -0.125 to 0.125
- shared_up: bfloat16 [2816, 2048], P('hid'), may hold values from -0.125 to 0.125
- shared_down: bfloat16 [2816, 2048], P('hid'), may hold values from -0.109375 to 0.109375
Outputs:
- layer_out: bfloat16 [2048, 2048], P('seq', 'hid')
The draws below stay inside these ranges and needn't reach their ends.
Inputs may be any that keep to these rules, and one draw needn't show every extreme that they name: `segment_ids`: segment numbers never fall along the tokens; every segment has at most 1024 tokens and one has exactly 1024. `expert_ids`: the 6 experts of a token differ; among the 512 tokens of one index of seq no expert is named by more than 64 tokens, a bound that some block reaches of them.
All inputs are finite; a program needn't handle non-finite values.
Results may differ from the reference program's by a relative error of at most 0.019.
Values may be sent and summed in bfloat16 or wider, within the bound.
A program may use at most 128 MiB of HBM per device.

```python
import math
import jax
import jax.numpy as jnp
import numpy as np
from jax import lax

D = 2048
HEADS = 16
HEAD_DIM = 128
EXPERTS = 64
FF = 1408
SHARED_FF = 2816
TOP = 6
TOK_SEQ = 512
SEGS = 4
TOKENS = 2048
LONGEST = 1024
CAP = 64
FF_PARTS = 1
N_SEQ = 4
N_HID = 8


def drawn_rows(key):
    base_key = jax.random.fold_in(key, 4099)
    key_base = jnp.clip(jax.random.normal(jax.random.fold_in(base_key, 3), (TOKENS, HEADS, HEAD_DIM), jnp.float32), -5.0, 5.0)
    return key_base


def draw_key_rows(key, part):
    key_base = drawn_rows(key)
    return key_base.astype(jnp.bfloat16)


def draw_queries(key, part):
    query_noise = jnp.clip(jax.random.normal(jax.random.fold_in(key, 7001), (TOKENS, HEADS, HEAD_DIM), jnp.float32), -4.0, 4.0) * 1.5
    return query_noise.astype(jnp.bfloat16)


def block_levels(own_key, dims, shards, least, high):
    gain = 1.0
    for axis_at, parts in shards:
        heights = jax.random.uniform(jax.random.fold_in(jax.random.fold_in(own_key, 6), axis_at), (parts,), jnp.float32, least / len(shards), high / len(shards))
        gain = gain * jnp.repeat(jnp.exp(heights), dims[axis_at] // parts).reshape((-1,) + (1,) * (len(dims) - 1 - axis_at))
    return gain


def profile(amount, total, reach, lean):
    portions = [(1 << 20) // math.isqrt(grade ** lean) + 1 for grade in range(2, amount + 1)]
    surplus, counts = total - reach - (amount - 1), [1] * (amount - 1)
    while surplus > 0:
        movable = [i for i in range(amount - 1) if counts[i] < reach]
        pool, budget = sum([portions[i] for i in movable]), surplus
        for i in movable:
            addition = min(reach - counts[i], max(1, budget * portions[i] // pool), surplus)
            counts[i] = counts[i] + addition
            surplus = surplus - addition
    return np.array([reach] + counts)


def uneven_parts(rng, amount, total, reach, lean):
    if amount == 2:
        one = jax.random.randint(rng, (), max(1, total - reach), min(reach, total - 1) + 1)
        return jnp.stack([one, total - one])
    sizes = jnp.asarray(profile(amount, total, reach, lean), jnp.int32)
    couples = (amount - 1) // 2
    donor, sink = sizes[1:1 + 2 * couples:2], sizes[2:2 + 2 * couples:2]
    slack = jnp.minimum(donor - 1, reach - sink)
    moved = jax.random.randint(jax.random.fold_in(rng, 1), (couples,), 0, 1 << 20) % (slack + 1)
    sizes = sizes.at[1:1 + 2 * couples:2].set(donor - moved).at[2:2 + 2 * couples:2].set(sink + moved)
    return sizes[jax.random.permutation(jax.random.fold_in(rng, 2), amount)]


def routed_block(rng, own, number, rows, number_of, top, most, slope):
    ranking = jax.random.permutation(rng, number_of)
    crowded, common = load_shares(number_of, rows * top, most, slope, True), load_shares(number_of, rows * top, most, slope, False)
    places = jnp.arange(number_of)

    def named(tallies, rotation):
        used = int((tallies > 0).sum())
        fixed = max(1, used // 4)
        shifted = fixed + (places - fixed + rotation * (used - fixed)) % max(1, number_of - fixed)
        return jnp.zeros((number_of,), jnp.int32).at[ranking[jnp.where(places < fixed, places, shifted)]].set(jnp.asarray(tallies, jnp.int32))

    tallies = jnp.where(number % 4 == 0, named(crowded, number // 4), named(common, number - number // 4 - 1))
    mixed = jax.random.permutation(jax.random.fold_in(own, 3), number_of)
    source_of, taker = mixed[0:number_of // 2 * 2:2], mixed[1:number_of // 2 * 2:2]
    slack = jnp.minimum(tallies[source_of] - 1, most - tallies[taker]) // 2
    slack = jnp.where((source_of == ranking[0]) | (taker == ranking[0]) | (tallies[taker] == 0), 0, jnp.maximum(slack, 0))
    shifted = jax.random.randint(jax.random.fold_in(own, 4), (number_of // 2,), 0, 1 << 20) % (slack + 1)
    tallies = tallies.at[source_of].add(-shifted).at[taker].add(shifted)
    members = jnp.searchsorted(jnp.cumsum(tallies), jnp.arange(rows * top), side="right").astype(jnp.int32)
    grid = members.reshape(top, rows).T
    grid = grid[jax.random.permutation(jax.random.fold_in(own, 1), rows)]
    rotation = jax.random.randint(jax.random.fold_in(own, 2), (rows, 1), 0, top)
    return jnp.take_along_axis(grid, (jnp.arange(top)[None, :] + rotation) % top, axis=1)


def load_shares(number_of, total, bound, slope, full):
    weights = [(1 << 20) // math.isqrt(rank ** slope) + 1 for rank in range(1, number_of + 1)]
    largest = bound if full else min(bound, max(-(-total // number_of), total * weights[0] // sum(weights)))
    least = 1 if total - largest >= number_of - 1 else 0
    counts, rest = [largest] + [least] * (number_of - 1), total - largest - least * (number_of - 1)
    while rest > 0:
        free = [i for i in range(1, number_of) if counts[i] < largest] or [i for i in range(1, number_of) if counts[i] < bound]
        whole, remaining = sum([weights[i] for i in free]), rest
        for i in free:
            more = min(bound - counts[i], max(1, remaining * weights[i] // whole), rest)
            counts[i] = counts[i] + more
            rest = rest - more
    return np.array(counts)


def bell_draw(stream_key, dims, deviation, most, cuts=(), kind=jnp.bfloat16):
    entries = jax.random.normal(stream_key, dims, jnp.float32) * deviation
    if len(cuts) > 0:
        entries = block_levels(stream_key, dims, cuts, -0.22, 0.18) * entries
    return jnp.clip(entries, min=-most, max=most).astype(kind)


def setup_inputs(seed: int = 0) -> dict:
    keys = jax.random.split(jax.random.key(seed), 16)
    stream = bell_draw(keys[0], (TOKENS, D), 1.0, 5.0, ((0, 4),))
    queries = draw_queries(jax.random.fold_in(keys[15], 71), 0)
    key_rows = draw_key_rows(jax.random.fold_in(keys[15], 71), 0)
    value_rows = bell_draw(keys[3], (TOKENS, HEADS, HEAD_DIM), 1.0, 5.0, ((0, 4), (1, 8)))
    segment_ids = jnp.searchsorted(jnp.cumsum(uneven_parts(keys[4], SEGS, TOKENS, LONGEST, 2)), jnp.arange(TOKENS), side="right").astype(jnp.int32)
    out_proj = bell_draw(keys[5], (HEADS, HEAD_DIM, D), (HEADS * HEAD_DIM) ** -0.5, 0.125, ((0, 8),))
    norm_gain = jnp.clip(1.0 + 0.18 * jax.random.normal(keys[6], (D,), jnp.float32), 0.1, 1.9)
    expert_ids_keys = jax.random.split(jax.random.fold_in(keys[7], 1), TOKENS // TOK_SEQ)
    expert_ids_turns = jax.random.permutation(jax.random.fold_in(keys[7], 3), TOKENS // TOK_SEQ)
    expert_ids = jax.vmap(lambda own, number: routed_block(jax.random.fold_in(keys[7], 2), own, number, TOK_SEQ, EXPERTS, TOP, CAP, 2))(expert_ids_keys, expert_ids_turns).reshape((TOKENS, TOP))
    route_gates = jnp.clip(0.05 + 0.35 * jax.random.uniform(keys[8], (TOKENS, TOP), jnp.float32) ** block_levels(keys[8], (TOKENS, TOP), ((0, 4),), -0.2, 0.2), 0.05, 0.4)
    gate_proj = bell_draw(keys[9], (EXPERTS * FF, D), D ** -0.5, 0.125, ((0, 32),))
    up_proj = bell_draw(keys[10], (EXPERTS * FF, D), D ** -0.5, 0.125, ((0, 32),))
    down_proj = bell_draw(keys[11], (EXPERTS * FF, D), FF ** -0.5, 0.15625, ((0, 32),))
    shared_gate = bell_draw(keys[12], (SHARED_FF, D), D ** -0.5, 0.125, ((0, 8),))
    shared_up = bell_draw(keys[13], (SHARED_FF, D), D ** -0.5, 0.125, ((0, 8),))
    shared_down = bell_draw(keys[14], (SHARED_FF, D), SHARED_FF ** -0.5, 0.109375, ((0, 8),))
    return {"stream": stream, "queries": queries, "key_rows": key_rows, "value_rows": value_rows, "segment_ids": segment_ids, "out_proj": out_proj, "norm_gain": norm_gain, "expert_ids": expert_ids, "route_gates": route_gates, "gate_proj": gate_proj, "up_proj": up_proj, "down_proj": down_proj, "shared_gate": shared_gate, "shared_up": shared_up, "shared_down": shared_down}


def grouped_down(acts, downs, group_total):
    row_count = acts.shape[0]
    group_width = acts.shape[1] // group_total
    act_groups = acts.reshape(row_count, group_total, group_width).transpose(1, 0, 2)
    down_groups = downs.reshape(group_total, group_width, downs.shape[1])

    def add_group(running, group_pair):
        part_out = jnp.dot(group_pair[0], group_pair[1], preferred_element_type=jnp.float32).astype(jnp.bfloat16)
        part_out = lax.optimization_barrier(part_out)
        return (running + part_out.astype(jnp.float32), None)
    running, ignored = lax.scan(add_group, jnp.zeros((row_count, downs.shape[1]), jnp.float32), (act_groups, down_groups))
    return running

def reference(stream, queries, key_rows, value_rows, segment_ids, out_proj, norm_gain, expert_ids, route_gates, gate_proj, up_proj, down_proj, shared_gate, shared_up, shared_down):
    positions = jnp.arange(TOKENS, dtype=jnp.int32)
    allowed = (segment_ids[:, None] == segment_ids[None, :]) & (positions[None, :] <= positions[:, None])
    inv_root = HEAD_DIM ** (-0.5)

    def attend_head(head_rows):
        query_head, key_head, value_head = head_rows
        scores = jnp.dot(query_head, key_head.T, preferred_element_type=jnp.float32) * inv_root
        scores = jnp.where(allowed, scores, -1e+30)
        row_top = lax.optimization_barrier(jnp.max(scores, axis=1, keepdims=True))
        weights = jnp.where(allowed, jnp.exp(scores - row_top), 0.0)
        totals = lax.optimization_barrier(jnp.sum(weights, axis=1, keepdims=True))
        probs = weights.astype(jnp.bfloat16)
        attended = jnp.dot(probs, value_head, preferred_element_type=jnp.float32) / totals
        return attended.astype(jnp.bfloat16)
    per_head = lax.map(attend_head, (queries.transpose(1, 0, 2), key_rows.transpose(1, 0, 2), value_rows.transpose(1, 0, 2)))
    attended = per_head.transpose(1, 0, 2).reshape(TOKENS, HEADS * HEAD_DIM)
    mixed = stream.astype(jnp.float32) + jnp.dot(attended, out_proj.reshape(HEADS * HEAD_DIM, D), preferred_element_type=jnp.float32)
    mean_square = lax.optimization_barrier(jnp.mean(mixed * mixed, axis=1, keepdims=True))
    normed = (mixed * lax.rsqrt(mean_square + 1e-06) * norm_gain).astype(jnp.bfloat16)
    shared_gate_val = jnp.dot(normed, shared_gate.T, preferred_element_type=jnp.float32)
    shared_up_val = jnp.dot(normed, shared_up.T, preferred_element_type=jnp.float32)
    shared_act = (jax.nn.silu(shared_gate_val) * shared_up_val).astype(jnp.bfloat16)
    shared_out = grouped_down(shared_act, shared_down, N_HID)
    flat_ids = expert_ids.reshape(N_SEQ, TOK_SEQ * TOP)
    onehot = (flat_ids[:, :, None] == jnp.arange(EXPERTS, dtype=jnp.int32)[None, None, :]).astype(jnp.int32)
    slot_rank = lax.optimization_barrier(jnp.sum((jnp.cumsum(onehot, axis=1) - 1) * onehot, axis=2)).astype(jnp.int32)
    block_index = jnp.arange(N_SEQ, dtype=jnp.int32)[:, None]
    slot_index = (flat_ids * (N_SEQ * CAP) + block_index * CAP + slot_rank).reshape(-1).astype(jnp.int32)
    expert_input = jnp.zeros((EXPERTS * N_SEQ * CAP, D), jnp.bfloat16).at[slot_index].set(jnp.repeat(normed, TOP, axis=0))
    expert_input = expert_input.reshape(EXPERTS, N_SEQ * CAP, D)

    def run_expert(expert_parts):
        rows_in, gate_one, up_one, down_one = expert_parts
        gate_val = jnp.dot(rows_in, gate_one.T, preferred_element_type=jnp.float32)
        up_val = jnp.dot(rows_in, up_one.T, preferred_element_type=jnp.float32)
        expert_act = (jax.nn.silu(gate_val) * up_val).astype(jnp.bfloat16)
        return grouped_down(expert_act, down_one, FF_PARTS).astype(jnp.bfloat16)
    expert_out = lax.map(run_expert, (expert_input, gate_proj.reshape(EXPERTS, FF, D), up_proj.reshape(EXPERTS, FF, D), down_proj.reshape(EXPERTS, FF, D)))
    picked = expert_out.reshape(EXPERTS * N_SEQ * CAP, D)[slot_index].reshape(TOKENS, TOP, D).astype(jnp.float32)
    routed = lax.optimization_barrier(jnp.sum(route_gates[:, :, None] * picked, axis=1))
    return (mixed + shared_out + routed).astype(jnp.bfloat16)
```

```python
import functools

import jax
import jax.numpy as jnp
from jax import lax
from jax.experimental import pallas as pl
from jax.experimental.pallas import tpu as pltpu
from jax.sharding import PartitionSpec as P

EXPERTS = 64
FF = 1408
TOP = 6
CAP = 64
HZ = 4
MESH = pl.DeviceIdType.MESH
F32 = jnp.float32
BF16 = jnp.bfloat16


def wrap(value, count):
    return lax.rem(value + count, count)


def remote(src, dst, send, recv, seq, hid):
    return pltpu.make_async_remote_copy(
        src_ref=src,
        dst_ref=dst,
        send_sem=send,
        recv_sem=recv,
        device_id=(seq, hid),
        device_id_type=MESH,
    )


def greet(seq, hid):
    pl.semaphore_signal(
        pltpu.get_barrier_semaphore(), inc=1, device_id=(seq, hid), device_id_type=MESH
    )


def mix_kernel(
    ns, hy, rows, slots, cols,
    att, wout, stream, gain, route, sg, su, sd,
    x_out, sh_out,
    ysend, yrecv, zsend, zrecv, normed, dsend, drecv, ssend, srecv, mixed,
    y_s, y_r, z_s, z_r, az_s, az_r, ay_s, ay_r, d_s, d_r, s_s, s_r,
):
    s = lax.axis_index("seq")
    h = lax.axis_index("hid")
    z, y = h // hy, lax.rem(h, hy)
    for dz in range(1, HZ):
        greet(s, wrap(z + dz, HZ) * hy + y)
    for dy in range(1, hy):
        greet(s, z * hy + wrap(y + dy, hy))
    for k in range(1, ns):
        greet(wrap(s + k, ns), h)
    pl.semaphore_wait(pltpu.get_barrier_semaphore(), HZ - 1 + hy - 1 + ns - 1)

    def at(c):
        return pl.ds(pl.multiple_of(c * rows, rows), rows)

    def part(c):
        return jnp.dot(att[at(c), :], wout[...], preferred_element_type=F32)

    sent = []
    for i in range(HZ):
        zt = wrap(z + i + 1, HZ)
        for j in range(hy - 1):
            yt = wrap(y + j + 1, hy)
            ysend[i, j] = part(zt * hy + yt).astype(BF16)
            copy = remote(ysend.at[i, j], yrecv.at[i, j], y_s.at[i, j], y_r.at[i, j], s, z * hy + yt)
            copy.start()
            sent.append(copy)
    to_y, to_z, acc = list(sent), [], None
    for i in range(HZ):
        zt = wrap(z + i + 1, HZ)
        acc = part(zt * hy + y)
        for j in range(hy - 1):
            to_y[i * (hy - 1) + j].wait_recv()
            acc = acc + yrecv[i, j].astype(F32)
        if i < HZ - 1:
            zsend[i] = acc.astype(BF16)
            copy = remote(zsend.at[i], zrecv.at[i], z_s.at[i], z_r.at[i], s, zt * hy + y)
            copy.start()
            to_z.append(copy)
    sent += to_z
    acc = acc + stream[...].astype(F32)
    for copy, i in zip(to_z, range(HZ)):
        copy.wait_recv()
        acc = acc + zrecv[i].astype(F32)
    mixed[...] = acc
    mean_square = jnp.mean(acc * acc, axis=1, keepdims=True)
    normed[at(h), :] = (acc * lax.rsqrt(mean_square + 1e-06) * gain[...]).astype(BF16)

    def spread(c, i):
        made = []
        for j in range(hy - 1):
            yt = wrap(y + j + 1, hy)
            copy = remote(normed.at[at(c)], normed.at[at(c)], ay_s.at[i, j], ay_r.at[i, j], s, z * hy + yt)
            copy.start()
            made.append(copy)
        return made

    gathers = []
    for i in range(HZ - 1):
        zt = wrap(z + i + 1, HZ)
        copy = remote(normed.at[at(h)], normed.at[at(h)], az_s.at[i], az_r.at[i], s, zt * hy + y)
        copy.start()
        gathers.append(copy)
    sides = spread(h, HZ - 1)
    for i in range(HZ - 1):
        c = wrap(z - i - 1, HZ) * hy + y
        remote(normed.at[at(c)], normed.at[at(c)], az_s.at[i], az_r.at[i], s, h).wait_recv()
        sides += spread(c, i)
    for i in range(HZ):
        for j in range(hy - 1):
            src = wrap(z - i - 1, HZ) * hy + wrap(y - j - 1, hy)
            remote(normed.at[at(src)], normed.at[at(src)], ay_s.at[i, j], ay_r.at[i, j], s, h).wait_recv()
    sent += gathers + sides

    def picked(block):
        rows_of = route[pl.ds(pl.multiple_of(block * slots, slots), slots), :]
        return jnp.dot(rows_of, normed[...], preferred_element_type=F32).astype(BF16)

    to_seq = []
    for k in range(ns - 1):
        kt = wrap(s + ns - 1 - k, ns)
        dsend[k] = picked(kt)
        copy = remote(dsend.at[k], drecv.at[k], d_s.at[k], d_r.at[k], kt, h)
        copy.start()
        to_seq.append(copy)
    sent += to_seq

    nt = (((1,), (1,)), ((), ()))
    gate_val = lax.dot_general(normed[...], sg[...], nt, preferred_element_type=F32)
    up_val = lax.dot_general(normed[...], su[...], nt, preferred_element_type=F32)
    act = (gate_val / (1.0 + jnp.exp(-gate_val)) * up_val).astype(BF16)

    def shared(hid, hold, at_hold):
        at_cols = pl.ds(pl.multiple_of(hid * cols, cols), cols)
        hold[at_hold] = jnp.dot(act, sd[:, at_cols], preferred_element_type=F32)
        hold[at_hold, at(h), :] = hold[at_hold, at(h), :] + mixed[:, at_cols]

    to_side = []
    for zt in range(HZ):
        for j in range(hy - 1):
            yt = wrap(y + j + 1, hy)
            shared(zt * hy + yt, sh_out, zt)
            ssend[zt, j] = sh_out[zt].astype(BF16)
            copy = remote(ssend.at[zt, j], srecv.at[zt, j], s_s.at[zt, j], s_r.at[zt, j], s, z * hy + yt)
            copy.start()
            to_side.append(copy)
    sent += to_side
    for zt in range(HZ):
        shared(zt * hy + y, sh_out, zt)
        for j in range(hy - 1):
            to_side[zt * (hy - 1) + j].wait_recv()
            sh_out[zt] = sh_out[zt] + srecv[zt, j].astype(F32)
    x_out[s] = picked(s)
    for k in range(ns - 1):
        to_seq[k].wait_recv()
        x_out[wrap(s + k + 1, ns)] = drecv[k]
    for copy in sent:
        copy.wait_send()


def combine_kernel(
    ns, hy, slots, cols,
    eo, gates, sh,
    out,
    recv, zsend, zrecv, l_s, l_r, z_s, z_r,
):
    s = lax.axis_index("seq")
    h = lax.axis_index("hid")
    z, y = h // hy, lax.rem(h, hy)
    layer = ns * hy
    me = s * hy + y

    def hello(k, carry):
        peer = lax.rem(me + k, layer)
        greet(peer // hy, z * hy + lax.rem(peer, hy))
        return carry

    lax.fori_loop(1, layer, hello, 0)
    for dz in range(1, HZ):
        greet(s, wrap(z + dz, HZ) * hy + y)
    pl.semaphore_wait(pltpu.get_barrier_semaphore(), layer - 1 + HZ - 1)

    def chunk(block, hid):
        return eo.at[block, :, pl.ds(pl.multiple_of(hid * cols, cols), cols)]

    def outgoing(i, k):
        zt = wrap(z + i + 1, HZ)
        peer = lax.rem(me + k, layer)
        block, yt = peer // hy, lax.rem(peer, hy)
        return remote(chunk(block, zt * hy + yt), recv.at[i, me], l_s.at[i, k], l_r.at[i, k], block, z * hy + yt)

    def incoming(i, k):
        peer = lax.rem(me + layer - k, layer)
        return remote(recv.at[i, peer], recv.at[i, peer], l_s.at[i, k], l_r.at[i, k], s, h)

    for i in range(HZ):
        def start(k, carry, i=i):
            outgoing(i, layer - k).start()
            return carry

        lax.fori_loop(1, layer, start, 0)
        recv[i, me] = eo[s, :, pl.ds(pl.multiple_of((wrap(z + i + 1, HZ) * hy + y) * cols, cols), cols)]

    to_z, total = [], None
    for i in range(HZ):
        def land(k, carry, i=i):
            incoming(i, layer - k).wait_recv()
            return carry

        lax.fori_loop(1, layer, land, 0)
        zt = wrap(z + i + 1, HZ)
        total = sh[zt] + jnp.dot(
            gates[...], recv[i].reshape(layer * slots, cols), preferred_element_type=F32
        )
        if i < HZ - 1:
            zsend[i] = total.astype(BF16)
            copy = remote(zsend.at[i], zrecv.at[i], z_s.at[i], z_r.at[i], s, zt * hy + y)
            copy.start()
            to_z.append(copy)
    for i in range(HZ - 1):
        to_z[i].wait_recv()
        total = total + zrecv[i].astype(F32)
    out[...] = total.astype(BF16)
    for i in range(HZ):
        def left(k, carry, i=i):
            outgoing(i, k).wait_send()
            return carry

        lax.fori_loop(1, layer, left, 0)
    for copy in to_z:
        copy.wait_send()


def on_device(
    stream,
    queries,
    key_rows,
    value_rows,
    segment_ids,
    out_proj,
    norm_gain,
    expert_ids,
    route_gates,
    gate_proj,
    up_proj,
    down_proj,
    shared_gate,
    shared_up,
    shared_down,
):
    tok_count, local_heads, head_width = queries.shape
    width = stream.shape[1]
    ns = lax.axis_size("seq")
    nh = lax.axis_size("hid")
    hy = nh // HZ
    rows = tok_count // nh
    cols = width // nh
    seq_index = lax.axis_index("seq")
    hid_index = lax.axis_index("hid")
    z_index = hid_index // hy
    unit_rows = gate_proj.shape[0]
    held = max(1, unit_rows // FF)
    units = unit_rows // held
    local_experts = EXPERTS // ns
    slots = held * CAP

    experts = jnp.arange(EXPERTS, dtype=jnp.int32)
    named = expert_ids[:, :, None] == experts[None, None, :]
    member = jnp.any(named, axis=1).astype(BF16)
    gate_of = jnp.sum(jnp.where(named, route_gates[:, :, None], 0.0), axis=1).astype(BF16)
    place = jnp.arange(tok_count, dtype=jnp.int32)
    earlier = (place[None, :] < place[:, None]).astype(BF16)
    rank = jnp.dot(earlier, member, preferred_element_type=F32)
    rank = jnp.where(member > 0, rank, 128.0).astype(BF16)
    slot = jnp.arange(CAP, dtype=jnp.int32).astype(F32)
    held_at = jnp.arange(held, dtype=jnp.int32)
    mine = (
        jnp.arange(ns, dtype=jnp.int32)[:, None] * local_experts
        + hid_index * unit_rows // FF
        + held_at[None, :]
    ).reshape(-1)
    pick_mine = (experts[:, None] == mine[None, :]).astype(BF16)
    rank_mine = lax.dot_general(
        pick_mine, rank, (((0,), (1,)), ((), ())), preferred_element_type=F32
    )
    route = (
        (rank_mine[:, None, :] == slot[None, :, None])
        .astype(BF16)
        .reshape(ns * slots, tok_count)
    )
    layer_hid = z_index * hy + jnp.arange(hy, dtype=jnp.int32)
    layer = (
        jnp.arange(ns, dtype=jnp.int32)[:, None, None] * local_experts
        + (layer_hid * unit_rows // FF)[None, :, None]
        + held_at[None, None, :]
    ).reshape(-1)
    pick_layer = (experts[:, None] == layer[None, :]).astype(BF16)
    rank_layer = jnp.dot(rank, pick_layer, preferred_element_type=F32)
    gate_layer = jnp.dot(gate_of, pick_layer, preferred_element_type=F32)
    gates = (
        jnp.where(rank_layer[:, :, None] == slot[None, None, :], gate_layer[:, :, None], 0.0)
        .astype(BF16)
        .reshape(tok_count, ns * hy * slots)
    )

    query_first = seq_index * tok_count
    query_seg = lax.dynamic_slice_in_dim(segment_ids, query_first, tok_count)
    query_pos = query_first + place
    both = jnp.concatenate([key_rows, value_rows], axis=1).reshape(tok_count, -1)
    both = lax.all_gather(both, "seq", axis=0, tiled=True)
    both = both.reshape(-1, 2 * local_heads, head_width)
    keys, values = both[:, :local_heads], both[:, local_heads:]
    key_pos = jnp.arange(keys.shape[0], dtype=jnp.int32)
    allowed = (query_seg[:, None] == segment_ids[None, :]) & (
        key_pos[None, :] <= query_pos[:, None]
    )
    scores = jnp.einsum("qhd,khd->qhk", queries, keys, preferred_element_type=F32)
    scores = jnp.where(allowed[:, None, :], scores * head_width**-0.5, -1e30)
    top = jnp.max(scores, axis=2)
    weights = jnp.where(allowed[:, None, :], jnp.exp(scores - top[:, :, None]), 0.0)
    totals = jnp.sum(weights, axis=2)
    mixed_values = jnp.einsum(
        "qhk,khd->qhd", weights.astype(BF16), values, preferred_element_type=F32
    )
    attended = (mixed_values / totals[:, :, None]).astype(BF16).reshape(tok_count, -1)

    vmem = pl.BlockSpec(memory_space=pltpu.VMEM)
    dma = pltpu.SemaphoreType.DMA
    own_stream = lax.dynamic_slice_in_dim(stream, hid_index * rows, rows)
    x, sh = pl.pallas_call(
        functools.partial(mix_kernel, ns, hy, rows, slots, cols),
        out_shape=(
            jax.ShapeDtypeStruct((ns, slots, width), BF16),
            jax.ShapeDtypeStruct((HZ, tok_count, cols), F32),
        ),
        in_specs=[vmem] * 8,
        out_specs=(vmem, vmem),
        scratch_shapes=[
            pltpu.VMEM((HZ, hy - 1, rows, width), BF16),
            pltpu.VMEM((HZ, hy - 1, rows, width), BF16),
            pltpu.VMEM((HZ - 1, rows, width), BF16),
            pltpu.VMEM((HZ - 1, rows, width), BF16),
            pltpu.VMEM((tok_count, width), BF16),
            pltpu.VMEM((ns - 1, slots, width), BF16),
            pltpu.VMEM((ns - 1, slots, width), BF16),
            pltpu.VMEM((HZ, hy - 1, tok_count, cols), BF16),
            pltpu.VMEM((HZ, hy - 1, tok_count, cols), BF16),
            pltpu.VMEM((rows, width), F32),
            dma((HZ, hy - 1)), dma((HZ, hy - 1)),
            dma((HZ - 1,)), dma((HZ - 1,)),
            dma((HZ - 1,)), dma((HZ - 1,)),
            dma((HZ, hy - 1)), dma((HZ, hy - 1)),
            dma((ns - 1,)), dma((ns - 1,)),
            dma((HZ, hy - 1)), dma((HZ, hy - 1)),
        ],
        compiler_params=pltpu.CompilerParams(
            collective_id=0, has_side_effects=True, vmem_limit_bytes=48 * 2**20
        ),
    )(
        attended,
        out_proj.reshape(local_heads * head_width, width),
        own_stream,
        norm_gain.reshape(1, width),
        route,
        shared_gate,
        shared_up,
        shared_down,
    )

    x = x.reshape(ns, held, CAP, width)
    gate_local = gate_proj.reshape(held, units, width)
    up_local = up_proj.reshape(held, units, width)
    down_local = down_proj.reshape(held, units, width)
    gate_val = jnp.einsum("sicd,ifd->sicf", x, gate_local, preferred_element_type=F32)
    up_val = jnp.einsum("sicd,ifd->sicf", x, up_local, preferred_element_type=F32)
    act = (jax.nn.silu(gate_val) * up_val).astype(BF16)
    eo = jnp.einsum("sicf,ifd->sicd", act, down_local, preferred_element_type=F32)
    eo = eo.astype(BF16).reshape(ns, slots, width)

    count = ns * hy
    return pl.pallas_call(
        functools.partial(combine_kernel, ns, hy, slots, cols),
        out_shape=jax.ShapeDtypeStruct((tok_count, cols), BF16),
        in_specs=[vmem] * 3,
        out_specs=vmem,
        scratch_shapes=[
            pltpu.VMEM((HZ, count, slots, cols), BF16),
            pltpu.VMEM((HZ - 1, tok_count, cols), BF16),
            pltpu.VMEM((HZ - 1, tok_count, cols), BF16),
            dma((HZ, count)), dma((HZ, count)),
            dma((HZ - 1,)), dma((HZ - 1,)),
        ],
        compiler_params=pltpu.CompilerParams(
            collective_id=1, has_side_effects=True, vmem_limit_bytes=48 * 2**20
        ),
    )(eo, gates, sh)


def solution(mesh):
    placed = (
        P("seq", None),
        P("seq", "hid", None),
        P("seq", "hid", None),
        P("seq", "hid", None),
        P(),
        P("hid", None, None),
        P(),
        P("seq", None),
        P("seq", None),
        P(("seq", "hid"), None),
        P(("seq", "hid"), None),
        P(("seq", "hid"), None),
        P("hid", None),
        P("hid", None),
        P("hid", None),
    )
    return jax.shard_map(
        on_device, mesh=mesh, in_specs=placed, out_specs=P("seq", "hid"), check_vma=False
    )
```

```python
import functools

import jax
import jax.numpy as jnp
from jax import lax
from jax.experimental import pallas as pl
from jax.experimental.pallas import tpu as pltpu
from jax.sharding import PartitionSpec as P

EXPERTS = 64
FF = 1408
TOP = 6
CAP = 64
HZ = 4
MESH = pl.DeviceIdType.MESH
F32 = jnp.float32
BF16 = jnp.bfloat16


def wrap(value, count):
    return lax.rem(value + count, count)


def remote(src, dst, send, recv, seq, hid):
    return pltpu.make_async_remote_copy(
        src_ref=src,
        dst_ref=dst,
        send_sem=send,
        recv_sem=recv,
        device_id=(seq, hid),
        device_id_type=MESH,
    )


def greet(seq, hid):
    pl.semaphore_signal(
        pltpu.get_barrier_semaphore(), inc=1, device_id=(seq, hid), device_id_type=MESH
    )


def mix_kernel(
    ns, hy, rows, slots, cols,
    att, wout, stream, gain, route, sg_hbm, su_hbm, sd_hbm,
    x_out, sh_out, ss_out,
    ysend, yrecv, zsend, zrecv, normed, dsend, drecv, mixed, sg, su, sd,
    y_s, y_r, z_s, z_r, az_s, az_r, ay_s, ay_r, d_s, d_r, w_s,
):
    s = lax.axis_index("seq")
    h = lax.axis_index("hid")
    z, y = h // hy, lax.rem(h, hy)
    loads = []
    for i, (src, dst) in enumerate(((sg_hbm, sg), (su_hbm, su), (sd_hbm, sd))):
        copy = pltpu.make_async_copy(src, dst, w_s.at[i])
        copy.start()
        loads.append(copy)
    for dz in range(1, HZ):
        greet(s, wrap(z + dz, HZ) * hy + y)
    for dy in range(1, hy):
        greet(s, z * hy + wrap(y + dy, hy))
    for k in range(1, ns):
        greet(wrap(s + k, ns), h)
    pl.semaphore_wait(pltpu.get_barrier_semaphore(), HZ - 1 + hy - 1 + ns - 1)

    def at(c):
        return pl.ds(pl.multiple_of(c * rows, rows), rows)

    def part(c):
        return jnp.dot(att[at(c), :], wout[...], preferred_element_type=F32)

    sent = []
    for i in range(HZ):
        zt = wrap(z + i + 1, HZ)
        for j in range(hy - 1):
            yt = wrap(y + j + 1, hy)
            ysend[i, j] = part(zt * hy + yt).astype(BF16)
            copy = remote(ysend.at[i, j], yrecv.at[i, j], y_s.at[i, j], y_r.at[i, j], s, z * hy + yt)
            copy.start()
            sent.append(copy)
    to_y, to_z, acc = list(sent), [], None
    for i in range(HZ):
        zt = wrap(z + i + 1, HZ)
        acc = part(zt * hy + y)
        for j in range(hy - 1):
            to_y[i * (hy - 1) + j].wait_recv()
            acc = acc + yrecv[i, j].astype(F32)
        if i < HZ - 1:
            zsend[i] = acc.astype(BF16)
            copy = remote(zsend.at[i], zrecv.at[i], z_s.at[i], z_r.at[i], s, zt * hy + y)
            copy.start()
            to_z.append(copy)
    sent += to_z
    acc = acc + stream[...].astype(F32)
    for copy, i in zip(to_z, range(HZ)):
        copy.wait_recv()
        acc = acc + zrecv[i].astype(F32)
    mixed[...] = acc
    mean_square = jnp.mean(acc * acc, axis=1, keepdims=True)
    normed[at(h), :] = (acc * lax.rsqrt(mean_square + 1e-06) * gain[...]).astype(BF16)

    def spread(c, i):
        made = []
        for j in range(hy - 1):
            yt = wrap(y + j + 1, hy)
            copy = remote(normed.at[at(c)], normed.at[at(c)], ay_s.at[i, j], ay_r.at[i, j], s, z * hy + yt)
            copy.start()
            made.append(copy)
        return made

    gathers = []
    for i in range(HZ - 1):
        zt = wrap(z + i + 1, HZ)
        copy = remote(normed.at[at(h)], normed.at[at(h)], az_s.at[i], az_r.at[i], s, zt * hy + y)
        copy.start()
        gathers.append(copy)
    sides = spread(h, HZ - 1)
    for i in range(HZ - 1):
        c = wrap(z - i - 1, HZ) * hy + y
        remote(normed.at[at(c)], normed.at[at(c)], az_s.at[i], az_r.at[i], s, h).wait_recv()
        sides += spread(c, i)
    for i in range(HZ):
        for j in range(hy - 1):
            src = wrap(z - i - 1, HZ) * hy + wrap(y - j - 1, hy)
            remote(normed.at[at(src)], normed.at[at(src)], ay_s.at[i, j], ay_r.at[i, j], s, h).wait_recv()
    sent += gathers + sides

    def picked(block):
        rows_of = route[pl.ds(pl.multiple_of(block * slots, slots), slots), :]
        return jnp.dot(rows_of, normed[...], preferred_element_type=F32).astype(BF16)

    to_seq = []
    for k in range(ns - 1):
        kt = wrap(s + ns - 1 - k, ns)
        dsend[k] = picked(kt)
        copy = remote(dsend.at[k], drecv.at[k], d_s.at[k], d_r.at[k], kt, h)
        copy.start()
        to_seq.append(copy)
    sent += to_seq

    nt = (((1,), (1,)), ((), ()))
    for copy in loads:
        copy.wait()
    gate_val = lax.dot_general(normed[...], sg[...], nt, preferred_element_type=F32)
    up_val = lax.dot_general(normed[...], su[...], nt, preferred_element_type=F32)
    act = (gate_val / (1.0 + jnp.exp(-gate_val)) * up_val).astype(BF16)

    def shared(hid, hold, at_hold):
        at_cols = pl.ds(pl.multiple_of(hid * cols, cols), cols)
        hold[at_hold] = jnp.dot(act, sd[:, at_cols], preferred_element_type=F32)
        hold[at_hold, at(h), :] = hold[at_hold, at(h), :] + mixed[:, at_cols]

    for zt in range(HZ):
        for j in range(hy - 1):
            shared(zt * hy + wrap(y + j + 1, hy), sh_out, zt)
            ss_out[zt, j] = sh_out[zt].astype(BF16)
        shared(zt * hy + y, sh_out, zt)

    def keep(block, value):
        for e in range(slots // CAP):
            x_out[e, pl.ds(pl.multiple_of(block * CAP, CAP), CAP), :] = value[e * CAP : (e + 1) * CAP]

    keep(s, picked(s))
    for k in range(ns - 1):
        to_seq[k].wait_recv()
        keep(wrap(s + k + 1, ns), drecv[k])
    for copy in sent:
        copy.wait_send()


def expert_kernel(
    ns, hy, held, units, cols,
    x, gates, sh, ss, gate_hbm, up_hbm, down_hbm,
    out,
    wg, wu, wd, act, eo, recv, zsend, zrecv, srecv,
    w_s, l_s, l_r, z_s, z_r, s_s, s_r,
):
    s = lax.axis_index("seq")
    h = lax.axis_index("hid")
    z, y = h // hy, lax.rem(h, hy)
    layer = ns * hy
    me = s * hy + y
    slots = held * CAP

    loads = []
    for e in range(held):
        span = pl.ds(e * units, units)
        for i, (src, dst) in enumerate(((gate_hbm, wg), (up_hbm, wu), (down_hbm, wd))):
            copy = pltpu.make_async_copy(src.at[span], dst.at[span], w_s.at[e, i])
            copy.start()
            loads.append(copy)

    def hello(k, carry):
        peer = lax.rem(me + k, layer)
        greet(peer // hy, z * hy + lax.rem(peer, hy))
        return carry

    lax.fori_loop(1, layer, hello, 0)
    for dz in range(1, HZ):
        greet(s, wrap(z + dz, HZ) * hy + y)
    pl.semaphore_wait(pltpu.get_barrier_semaphore(), layer - 1 + HZ - 1)

    to_side = []
    for i in range(HZ):
        zt = wrap(z + i + 1, HZ)
        for j in range(hy - 1):
            copy = remote(
                ss.at[zt, j], srecv.at[i, j], s_s.at[i, j], s_r.at[i, j],
                s, z * hy + wrap(y + j + 1, hy),
            )
            copy.start()
            to_side.append(copy)

    nt = (((1,), (1,)), ((), ()))
    for e in range(held):
        loads[3 * e].wait()
        loads[3 * e + 1].wait()

        def hidden(first, size, e=e):
            span = pl.ds(e * units + first, size)
            gate_val = lax.dot_general(x[e], wg[span, :], nt, preferred_element_type=F32)
            up_val = lax.dot_general(x[e], wu[span, :], nt, preferred_element_type=F32)
            value = gate_val / (1.0 + jnp.exp(-gate_val)) * up_val
            act[e, :, pl.ds(first, size)] = value.astype(BF16)

        def tile(n, carry, hidden=hidden):
            hidden(pl.multiple_of(n * 256, 128), 256)
            return carry

        lax.fori_loop(0, units // 256, tile, 0)
        if units % 256:
            hidden(units // 256 * 256, units % 256)
    for e in range(held):
        loads[3 * e + 2].wait()

    def outgoing(i, j, k):
        block, yt = lax.rem(s + k, ns), wrap(y + j, hy)
        return remote(
            eo.at[i, j, block], recv.at[i, me], l_s.at[i, j, k], l_r.at[i, j, k],
            block, z * hy + yt,
        )

    def incoming(i, j, k):
        peer = lax.rem(s + ns - k, ns) * hy + wrap(y - j, hy)
        return remote(recv.at[i, peer], recv.at[i, peer], l_s.at[i, j, k], l_r.at[i, j, k], s, h)

    def every(action, i, j):
        def one(k, carry):
            action(i, j, k)
            return carry

        lax.fori_loop(1 if j == 0 else 0, ns, one, 0)

    for i in range(HZ):
        zt = wrap(z + i + 1, HZ)
        for j in reversed(range(hy)):
            hid = zt * hy + wrap(y + j, hy)
            span = pl.ds(pl.multiple_of(hid * cols, cols), cols)
            for e in range(held):
                value = jnp.dot(
                    act[e], wd[pl.ds(e * units, units), span], preferred_element_type=F32
                )
                eo[i, j, :, e * CAP : (e + 1) * CAP, :] = value.astype(BF16).reshape(ns, CAP, cols)
            every(lambda i, j, k: outgoing(i, j, k).start(), i, j)
        recv[i, me] = eo[i, 0, s]

    to_z, total = [], None
    for i in range(HZ):
        zt = wrap(z + i + 1, HZ)
        total = sh[zt]
        for j in range(hy - 1):
            to_side[i * (hy - 1) + j].wait_recv()
            total = total + srecv[i, j].astype(F32)
        for j in range(hy):
            every(lambda i, j, k: incoming(i, j, k).wait_recv(), i, j)
        total = total + jnp.dot(
            gates[...], recv[i].reshape(layer * slots, cols), preferred_element_type=F32
        )
        if i < HZ - 1:
            zsend[i] = total.astype(BF16)
            copy = remote(zsend.at[i], zrecv.at[i], z_s.at[i], z_r.at[i], s, zt * hy + y)
            copy.start()
            to_z.append(copy)
    for i in range(HZ - 1):
        to_z[i].wait_recv()
        total = total + zrecv[i].astype(F32)
    out[...] = total.astype(BF16)
    for i in range(HZ):
        for j in range(hy):
            every(lambda i, j, k: outgoing(i, j, k).wait_send(), i, j)
    for copy in to_z + to_side:
        copy.wait_send()


def on_device(
    stream,
    queries,
    key_rows,
    value_rows,
    segment_ids,
    out_proj,
    norm_gain,
    expert_ids,
    route_gates,
    gate_proj,
    up_proj,
    down_proj,
    shared_gate,
    shared_up,
    shared_down,
):
    tok_count, local_heads, head_width = queries.shape
    width = stream.shape[1]
    ns = lax.axis_size("seq")
    nh = lax.axis_size("hid")
    hy = nh // HZ
    rows = tok_count // nh
    cols = width // nh
    seq_index = lax.axis_index("seq")
    hid_index = lax.axis_index("hid")
    z_index = hid_index // hy
    unit_rows = gate_proj.shape[0]
    held = max(1, unit_rows // FF)
    units = unit_rows // held
    local_experts = EXPERTS // ns
    slots = held * CAP

    experts = jnp.arange(EXPERTS, dtype=jnp.int32)
    named = expert_ids[:, :, None] == experts[None, None, :]
    member = jnp.any(named, axis=1).astype(BF16)
    gate_of = jnp.sum(jnp.where(named, route_gates[:, :, None], 0.0), axis=1).astype(BF16)
    place = jnp.arange(tok_count, dtype=jnp.int32)
    earlier = (place[None, :] < place[:, None]).astype(BF16)
    rank = jnp.dot(earlier, member, preferred_element_type=F32)
    rank = jnp.where(member > 0, rank, 128.0).astype(BF16)
    slot = jnp.arange(CAP, dtype=jnp.int32).astype(F32)
    held_at = jnp.arange(held, dtype=jnp.int32)
    mine = (
        jnp.arange(ns, dtype=jnp.int32)[:, None] * local_experts
        + hid_index * unit_rows // FF
        + held_at[None, :]
    ).reshape(-1)
    pick_mine = (experts[:, None] == mine[None, :]).astype(BF16)
    rank_mine = lax.dot_general(
        pick_mine, rank, (((0,), (1,)), ((), ())), preferred_element_type=F32
    )
    route = (
        (rank_mine[:, None, :] == slot[None, :, None])
        .astype(BF16)
        .reshape(ns * slots, tok_count)
    )
    layer_hid = z_index * hy + jnp.arange(hy, dtype=jnp.int32)
    layer = (
        jnp.arange(ns, dtype=jnp.int32)[:, None, None] * local_experts
        + (layer_hid * unit_rows // FF)[None, :, None]
        + held_at[None, None, :]
    ).reshape(-1)
    pick_layer = (experts[:, None] == layer[None, :]).astype(BF16)
    rank_layer = jnp.dot(rank, pick_layer, preferred_element_type=F32)
    gate_layer = jnp.dot(gate_of, pick_layer, preferred_element_type=F32)
    gates = (
        jnp.where(rank_layer[:, :, None] == slot[None, None, :], gate_layer[:, :, None], 0.0)
        .astype(BF16)
        .reshape(tok_count, ns * hy * slots)
    )

    query_first = seq_index * tok_count
    query_seg = lax.dynamic_slice_in_dim(segment_ids, query_first, tok_count)
    query_pos = query_first + place
    both = jnp.concatenate([key_rows, value_rows], axis=1).reshape(tok_count, -1)
    both = lax.all_gather(both, "seq", axis=0, tiled=True)
    both = both.reshape(-1, 2 * local_heads, head_width)
    keys, values = both[:, :local_heads], both[:, local_heads:]
    key_pos = jnp.arange(keys.shape[0], dtype=jnp.int32)
    allowed = (query_seg[:, None] == segment_ids[None, :]) & (
        key_pos[None, :] <= query_pos[:, None]
    )
    scores = jnp.einsum("qhd,khd->qhk", queries, keys, preferred_element_type=F32)
    scores = jnp.where(allowed[:, None, :], scores * head_width**-0.5, -1e30)
    top = jnp.max(scores, axis=2)
    weights = jnp.where(allowed[:, None, :], jnp.exp(scores - top[:, :, None]), 0.0)
    totals = jnp.sum(weights, axis=2)
    mixed_values = jnp.einsum(
        "qhk,khd->qhd", weights.astype(BF16), values, preferred_element_type=F32
    )
    attended = (mixed_values / totals[:, :, None]).astype(BF16).reshape(tok_count, -1)

    vmem = pl.BlockSpec(memory_space=pltpu.VMEM)
    hbm = pl.BlockSpec(memory_space=pl.ANY)
    dma = pltpu.SemaphoreType.DMA
    own_stream = lax.dynamic_slice_in_dim(stream, hid_index * rows, rows)
    x, sh, ss = pl.pallas_call(
        functools.partial(mix_kernel, ns, hy, rows, slots, cols),
        out_shape=(
            jax.ShapeDtypeStruct((held, ns * CAP, width), BF16),
            jax.ShapeDtypeStruct((HZ, tok_count, cols), F32),
            jax.ShapeDtypeStruct((HZ, hy - 1, tok_count, cols), BF16),
        ),
        in_specs=[vmem] * 5 + [hbm] * 3,
        out_specs=(vmem, vmem, vmem),
        scratch_shapes=[
            pltpu.VMEM((HZ, hy - 1, rows, width), BF16),
            pltpu.VMEM((HZ, hy - 1, rows, width), BF16),
            pltpu.VMEM((HZ - 1, rows, width), BF16),
            pltpu.VMEM((HZ - 1, rows, width), BF16),
            pltpu.VMEM((tok_count, width), BF16),
            pltpu.VMEM((ns - 1, slots, width), BF16),
            pltpu.VMEM((ns - 1, slots, width), BF16),
            pltpu.VMEM((rows, width), F32),
            pltpu.VMEM(shared_gate.shape, BF16),
            pltpu.VMEM(shared_up.shape, BF16),
            pltpu.VMEM(shared_down.shape, BF16),
            dma((HZ, hy - 1)), dma((HZ, hy - 1)),
            dma((HZ - 1,)), dma((HZ - 1,)),
            dma((HZ - 1,)), dma((HZ - 1,)),
            dma((HZ, hy - 1)), dma((HZ, hy - 1)),
            dma((ns - 1,)), dma((ns - 1,)), dma((3,)),
        ],
        compiler_params=pltpu.CompilerParams(
            collective_id=0, has_side_effects=True, vmem_limit_bytes=48 * 2**20
        ),
    )(
        attended,
        out_proj.reshape(local_heads * head_width, width),
        own_stream,
        norm_gain.reshape(1, width),
        route,
        shared_gate,
        shared_up,
        shared_down,
    )

    count = ns * hy
    return pl.pallas_call(
        functools.partial(expert_kernel, ns, hy, held, units, cols),
        out_shape=jax.ShapeDtypeStruct((tok_count, cols), BF16),
        in_specs=[vmem] * 4 + [hbm] * 3,
        out_specs=vmem,
        scratch_shapes=[
            pltpu.VMEM((unit_rows, width), BF16),
            pltpu.VMEM((unit_rows, width), BF16),
            pltpu.VMEM((unit_rows, width), BF16),
            pltpu.VMEM((held, ns * CAP, units), BF16),
            pltpu.VMEM((HZ, hy, ns, slots, cols), BF16),
            pltpu.VMEM((HZ, count, slots, cols), BF16),
            pltpu.VMEM((HZ - 1, tok_count, cols), BF16),
            pltpu.VMEM((HZ - 1, tok_count, cols), BF16),
            pltpu.VMEM((HZ, hy - 1, tok_count, cols), BF16),
            dma((held, 3)),
            dma((HZ, hy, ns)), dma((HZ, hy, ns)),
            dma((HZ - 1,)), dma((HZ - 1,)),
            dma((HZ, hy - 1)), dma((HZ, hy - 1)),
        ],
        compiler_params=pltpu.CompilerParams(
            collective_id=1, has_side_effects=True, vmem_limit_bytes=58 * 2**20
        ),
    )(x, gates, sh, ss, gate_proj, up_proj, down_proj)


def solution(mesh):
    placed = (
        P("seq", None),
        P("seq", "hid", None),
        P("seq", "hid", None),
        P("seq", "hid", None),
        P(),
        P("hid", None, None),
        P(),
        P("seq", None),
        P("seq", None),
        P(("seq", "hid"), None),
        P(("seq", "hid"), None),
        P(("seq", "hid"), None),
        P("hid", None),
        P("hid", None),
        P("hid", None),
    )
    return jax.shard_map(
        on_device, mesh=mesh, in_specs=placed, out_specs=P("seq", "hid"), check_vma=False
    )
```
